32 devices in a mesh: role: 2 (over core), dp: 4 (over z), vocab: 4 (over y, x).
Axes of the slice: x: 2, y: 2, z: 4, core: 2. Of those that a mesh axis runs over, the one named last changes fastest.
Arguments:
- teacher_hidden: bfloat16 [256, 4608], P('dp', ('role', 'vocab'))
- student_hidden: bfloat16 [256, 4096], P('dp', ('role', 'vocab'))
- teacher_unembed: bfloat16 [4608, 16384], P('role', ('dp', 'vocab')), may hold values from -6 to 6
- student_unembed: bfloat16 [4096, 16384], P('role', ('dp', 'vocab')), may hold values from -6 to 6
- targets: int32 [256], replicated, may hold values from 0 to 16383
Outputs:
- row_loss: float32 [256], replicated
- mean_loss: float32 [], replicated
- grad_hidden: float32 [256, 4096], P('dp', ('role', 'vocab'))
The draws below stay inside these ranges and needn't reach their ends.
All inputs are finite; a program needn't handle non-finite values.
Results may differ from the reference program's by a relative error of at most 0.0017.
Values may be sent and summed in bfloat16 or wider, within the bound.
A program may use at most 64 MiB of HBM per device.

```python
import math
import jax
import jax.numpy as jnp
import numpy as np

DT = 4608
DS = 4096
VOCAB = 16384
TOKENS = 256


def scaled_rows(key, rows, cols):
    first = jax.random.fold_in(key, 0)
    values = jax.random.normal(first, (rows, cols), jnp.float32) * (3.0 / math.sqrt(cols))
    return values.astype(jnp.bfloat16)


def draw_teacher_hidden(key, part):
    key = jax.random.fold_in(key, 11)
    return scaled_rows(key, TOKENS, DT)


def draw_student_hidden(key, part):
    key = jax.random.fold_in(key, 23)
    return scaled_rows(key, TOKENS, DS)


def touch_ends(values, key, smallest, largest):
    spot = [jax.random.randint(jax.random.fold_in(key, axis), (), 0, length) for axis, length in enumerate(values.shape)]
    widest = values.shape.index(max(values.shape))
    neighbour = spot[:widest] + [(spot[widest] + 1) % values.shape[widest]] + spot[widest + 1:]
    return values.at[tuple(spot)].set(smallest).at[tuple(neighbour)].set(largest)


def block_levels(rng, dims, cuts, smallest, top_value):
    def one(axis_at, blocks):
        heights = jax.random.uniform(jax.random.fold_in(jax.random.fold_in(rng, 6), axis_at), (blocks,), jnp.float32, smallest / len(cuts), top_value / len(cuts))
        return jnp.repeat(jnp.exp(heights), dims[axis_at] // blocks).reshape((-1,) + (1,) * (len(dims) - axis_at - 1))

    level = one(*cuts[0])
    for cut in cuts[1:]:
        level = level * one(*cut)
    return level


def cumulative_ranks(count, slope):
    loads = [(1 << 20) // math.isqrt(standing ** slope) + 1 for standing in range(1, count + 1)]
    scale = 1 + sum(loads) // (1 << 30)
    return np.cumsum(np.array([max(1, weight // scale) for weight in loads]))


def skewed_ids(stream_key, extent, amount, lean):
    table = cumulative_ranks(amount, lean)
    lot = jax.random.randint(jax.random.fold_in(stream_key, 1), extent, 0, int(table[amount - 1]))
    standing = jnp.searchsorted(jnp.asarray(table, jnp.int32), lot, side="right")
    return jax.random.permutation(jax.random.fold_in(stream_key, 2), amount)[standing].astype(jnp.int32)


def normal_values(stream_key, extent, scale, reach, shards=(), held_as=jnp.bfloat16):
    values = scale * jax.random.normal(stream_key, extent, jnp.float32)
    if shards:
        values = values * block_levels(stream_key, extent, shards, -0.22, 0.18)
    return jnp.clip(values, -reach, reach).astype(held_as)


def setup_inputs(seed: int = 0) -> dict:
    arg_keys = jax.random.split(jax.random.key(seed), 6)
    teacher_hidden = draw_teacher_hidden(jax.random.fold_in(arg_keys[5], 71), 0)
    student_hidden = draw_student_hidden(jax.random.fold_in(arg_keys[5], 71), 0)
    teacher_unembed = normal_values(arg_keys[2], (DT, VOCAB), 1.0, 6.0, ((0, 2), (1, 16)))
    student_unembed = normal_values(arg_keys[3], (DS, VOCAB), 1.0, 6.0, ((0, 2), (1, 16)))
    targets = touch_ends(skewed_ids(arg_keys[4], (TOKENS,), VOCAB, 2), jax.random.fold_in(arg_keys[4], 3), 0, VOCAB - 1).astype(jnp.int32)
    return dict(teacher_hidden=teacher_hidden, student_hidden=student_hidden, teacher_unembed=teacher_unembed, student_unembed=student_unembed, targets=targets)


def reference(teacher_hidden, student_hidden, teacher_unembed, student_unembed, targets):
    teacher_logits = jnp.dot(teacher_hidden, teacher_unembed, preferred_element_type=jnp.float32)
    student_logits = jnp.dot(student_hidden, student_unembed, preferred_element_type=jnp.float32)
    teacher_logp = jax.nn.log_softmax(teacher_logits, axis=1)
    student_logp = jax.nn.log_softmax(student_logits, axis=1)
    column = jnp.arange(VOCAB, dtype=jnp.int32)
    onehot = (column[None, :] == targets[:, None]).astype(jnp.float32)
    teacher_prob = jnp.exp(teacher_logp)
    student_prob = jnp.exp(student_logp)
    row_loss = jnp.sum(teacher_prob * (teacher_logp - student_logp) - onehot * student_logp, axis=1)
    mean_loss = jnp.mean(row_loss)
    logit_grad = (2.0 * student_prob - teacher_prob - onehot).astype(jnp.bfloat16)
    grad_hidden = jnp.dot(logit_grad, student_unembed.T, preferred_element_type=jnp.float32)
    return row_loss, mean_loss, grad_hidden
```

```python
import functools

import jax
import jax.numpy as jnp
from jax import lax
from jax.experimental import pallas as pl
from jax.experimental.pallas import tpu as pltpu
from jax.sharding import PartitionSpec as P

MESH = pl.DeviceIdType.MESH
TILE = 256
ROW_STEP = 32
LANES = 128


def flipped(index, bits, size):
    out, bit = index, 1
    while bit < size:
        if bits & bit:
            out = out + bit * (1 - 2 * lax.rem(lax.div(index, bit), 2))
        bit *= 2
    return out


def kernel(
    dp_size, vocab_size,
    th_ref, sh_ref, tw_ref, sw_ref, targets_ref,
    loss_ref, mean_ref, grad_ref,
    th, sh, tw, sw, t_acc, s_acc, t_other, s_other, target_col, stat_col, stats, losses, lse_col,
    logit_grad, term, from_vocab, to_dp, from_dp,
    local_sem, t_send, t_recv, s_send, s_recv, role_send, role_recv,
    stat_send, stat_recv, v_send, v_recv, d_send, d_recv,
):
    role, dp, vocab = lax.axis_index("role"), lax.axis_index("dp"), lax.axis_index("vocab")
    group = dp_size * vocab_size
    me = dp * vocab_size + vocab
    cols = tw.shape[1]
    block_rows = th_ref.shape[0]
    rows = dp_size * block_rows
    half = rows // 2
    features = sh_ref.shape[1]
    dps = [flipped(dp, k, dp_size) for k in range(dp_size)]
    vocabs = [flipped(vocab, k, vocab_size) for k in range(vocab_size)]
    partner = (1 - role, dp, vocab)
    sent = []

    def send(src, dst, send_sem, recv_sem, device):
        copy = pltpu.make_async_remote_copy(
            src_ref=src, dst_ref=dst, send_sem=send_sem, recv_sem=recv_sem,
            device_id=device, device_id_type=MESH,
        )
        copy.start()
        sent.append(copy)

    def arrived(dst, send_sem, recv_sem):
        pltpu.make_async_remote_copy(
            src_ref=dst, dst_ref=dst, send_sem=send_sem, recv_sem=recv_sem,
            device_id=partner, device_id_type=MESH,
        ).wait_recv()

    tw_copy = pltpu.make_async_copy(tw_ref, tw, local_sem.at[0])
    sw_copy = pltpu.make_async_copy(sw_ref, sw, local_sem.at[1])
    th_copy = pltpu.make_async_copy(th_ref, th.at[vocab, dp], local_sem.at[2])
    sh_copy = pltpu.make_async_copy(sh_ref, sh.at[vocab, dp], local_sem.at[3])
    for copy in (th_copy, sh_copy, tw_copy, sw_copy):
        copy.start()

    barrier = pltpu.get_barrier_semaphore()

    @pl.loop(1, group)
    def _(step):
        other = lax.rem(me + step, group)
        pl.semaphore_signal(
            barrier, inc=1,
            device_id=(role, lax.div(other, vocab_size), lax.rem(other, vocab_size)),
            device_id_type=MESH,
        )

    pl.semaphore_signal(barrier, inc=1, device_id=partner, device_id_type=MESH)
    pl.semaphore_wait(barrier, group)

    parts = ((th_ref, th, t_send, t_recv), (sh_ref, sh, s_send, s_recv))
    for source, held, send_sem, recv_sem in parts:
        for k in range(1, dp_size):
            send(
                source, held.at[vocab, dp], send_sem.at[0, k], recv_sem.at[vocab, dp],
                (role, dps[k], vocab),
            )
        for k in range(1, vocab_size):
            send(
                source, held.at[vocab, dp], send_sem.at[k, 0], recv_sem.at[vocab, dp],
                (role, dp, vocabs[k]),
            )

    target_col[...] = jnp.transpose(jnp.broadcast_to(targets_ref[...], (LANES, rows)))

    def pass_on(held, send_sem, recv_sem):
        for j in range(1, dp_size):
            slot = held.at[vocab, dps[j]]
            arrived(slot, send_sem.at[0, 0], recv_sem.at[vocab, dps[j]])
            for k in range(1, vocab_size):
                send(
                    slot, slot, send_sem.at[k, j], recv_sem.at[vocab, dps[j]],
                    (role, dp, vocabs[k]),
                )

    def add_product(held, weights, acc, k):
        depth = held.shape[-1]
        start = pl.multiple_of(vocabs[k] * depth, 16)

        @pl.loop(0, cols // TILE)
        def _(n):
            at = pl.ds(pl.multiple_of(n * TILE, TILE), TILE)
            product = jnp.dot(
                held[vocabs[k]].reshape(rows, depth),
                weights[pl.ds(start, depth), at],
                preferred_element_type=jnp.float32,
            )
            if k == 0:
                acc[:, at] = product
            else:
                acc[:, at] += product

    def add_arriving(held, weights, acc, send_sem, recv_sem):
        for k in range(1, vocab_size):
            for j in range(dp_size):
                arrived(
                    held.at[vocabs[k], dps[j]], send_sem.at[0, 0], recv_sem.at[vocabs[k], dps[j]]
                )
            add_product(held, weights, acc, k)

    own_rows = pl.multiple_of(role * half, ROW_STEP)
    other_rows = pl.multiple_of((1 - role) * half, ROW_STEP)

    pass_on(th, t_send, t_recv)
    th_copy.wait()
    tw_copy.wait()
    add_product(th, tw, t_acc, 0)
    pass_on(sh, s_send, s_recv)
    sh_copy.wait()
    sw_copy.wait()
    add_product(sh, sw, s_acc, 0)
    add_arriving(th, tw, t_acc, t_send, t_recv)
    send(t_acc.at[pl.ds(other_rows, half)], t_other, role_send.at[0], role_recv.at[0], partner)
    add_arriving(sh, sw, s_acc, s_send, s_recv)
    send(s_acc.at[pl.ds(other_rows, half)], s_other, role_send.at[1], role_recv.at[1], partner)
    arrived(t_other, role_send.at[0], role_recv.at[0])
    arrived(s_other, role_send.at[1], role_recv.at[1])

    column = lax.broadcasted_iota(jnp.int32, (ROW_STEP, cols), 1) + me * cols
    lane = lax.broadcasted_iota(jnp.int32, (ROW_STEP, LANES), 1)

    def at_rows(step):
        local = pl.ds(pl.multiple_of(step * ROW_STEP, ROW_STEP), ROW_STEP)
        whole = pl.ds(pl.multiple_of(own_rows + step * ROW_STEP, ROW_STEP), ROW_STEP)
        return local, whole

    @pl.loop(0, half // ROW_STEP)
    def _(step):
        local, whole = at_rows(step)
        teacher = t_acc[whole, :] + t_other[local, :]
        student = s_acc[whole, :] + s_other[local, :]
        hit = column == target_col[whole, 0:1]
        t_top = jnp.max(teacher, axis=1, keepdims=True)
        s_top = jnp.max(student, axis=1, keepdims=True)
        t_exp = jnp.exp(teacher - t_top)
        t_sum = jnp.sum(t_exp, axis=1, keepdims=True)
        gap = jnp.sum(t_exp * (teacher - student), axis=1, keepdims=True)
        s_sum = jnp.sum(jnp.exp(student - s_top), axis=1, keepdims=True)
        label = jnp.sum(jnp.where(hit, student, 0.0), axis=1, keepdims=True)
        packed = jnp.zeros((ROW_STEP, LANES), jnp.float32)
        for place, value in enumerate((t_top, t_sum, gap, s_top, s_sum, label)):
            packed = jnp.where(lane == place, value, packed)
        stat_col[local, :] = packed

    stats[me] = jnp.transpose(stat_col[...])[0:8, :]

    def stat_copy(step):
        other = lax.rem(me + step, group)
        return pltpu.make_async_remote_copy(
            src_ref=stats.at[me], dst_ref=stats.at[me],
            send_sem=stat_send.at[step], recv_sem=stat_recv.at[me],
            device_id=(role, lax.div(other, vocab_size), lax.rem(other, vocab_size)),
            device_id_type=MESH,
        )

    @pl.loop(1, group)
    def _(step):
        stat_copy(step).start()

    @pl.loop(1, group)
    def _(step):
        other = lax.rem(me + step, group)
        arrived(stats.at[other], stat_send.at[0], stat_recv.at[other])

    everyone = stats[...]
    t_top, t_sum, gap = everyone[:, 0, :], everyone[:, 1, :], everyone[:, 2, :]
    s_top, s_sum, label = everyone[:, 3, :], everyone[:, 4, :], everyone[:, 5, :]
    t_max = jnp.max(t_top, axis=0, keepdims=True)
    s_max = jnp.max(s_top, axis=0, keepdims=True)
    t_scale = jnp.exp(t_top - t_max)
    t_total = jnp.sum(t_sum * t_scale, axis=0, keepdims=True)
    s_total = jnp.sum(s_sum * jnp.exp(s_top - s_max), axis=0, keepdims=True)
    t_lse = t_max + jnp.log(t_total)
    s_lse = s_max + jnp.log(s_total)
    mean_gap = jnp.sum(gap * t_scale, axis=0, keepdims=True) / t_total
    s_label = jnp.sum(label, axis=0, keepdims=True)
    loss = (mean_gap - t_lse + s_lse) - (s_label - s_lse)
    losses[role] = jnp.broadcast_to(loss, (8, half))
    send(losses.at[role], losses.at[role], role_send.at[2], role_recv.at[2], partner)
    first = lax.broadcasted_iota(jnp.int32, (LANES, half), 0) == 0
    lse_col[...] = jnp.transpose(jnp.where(first, t_lse, s_lse))

    @pl.loop(0, half // ROW_STEP)
    def _(step):
        local, whole = at_rows(step)
        teacher = t_acc[whole, :] + t_other[local, :]
        student = s_acc[whole, :] + s_other[local, :]
        onehot = jnp.where(column == target_col[whole, 0:1], 1.0, 0.0)
        t_prob = jnp.exp(teacher - lse_col[local, 0:1])
        s_prob = jnp.exp(student - lse_col[local, 1:2])
        logit_grad[whole, :] = (2.0 * s_prob - t_prob - onehot).astype(jnp.bfloat16)

    mine = logit_grad.at[pl.ds(own_rows, half)]
    send(mine, mine, role_send.at[3], role_recv.at[3], partner)
    arrived(logit_grad.at[pl.ds(other_rows, half)], role_send.at[3], role_recv.at[3])

    def block(j):
        return pl.ds(pl.multiple_of(dps[j] * block_rows, block_rows), block_rows)

    def send_term(k, j):
        send(
            term.at[k, block(j)], from_vocab.at[k, block(j)],
            v_send.at[k, j], v_recv.at[k, dps[j]], (role, dp, vocabs[k]),
        )

    width = min(TILE, features)
    order = list(range(vocab_size - 1, -1, -1))
    far = list(range(dp_size - 1, -1, -1))
    for k in order:
        @pl.loop(0, features // width)
        def _(n):
            start = pl.multiple_of(vocabs[k] * features + n * width, width)
            term[k, :, pl.ds(pl.multiple_of(n * width, width), width)] = lax.dot_general(
                logit_grad[...], sw[pl.ds(start, width), :],
                (((1,), (1,)), ((), ())), preferred_element_type=jnp.float32,
            )
        if k:
            send_term(k, far[0])
    for j in far[1:]:
        for k in order[:-1]:
            send_term(k, j)
    for j in far:
        total = term[0, block(j), :]
        for k in order[:-1]:
            arrived(from_vocab.at[k, block(j)], v_send.at[0, 0], v_recv.at[k, dps[j]])
            total = total + from_vocab[k, block(j), :]
        to_dp[j] = total
        if j:
            send(to_dp.at[j], from_dp.at[j], d_send.at[j], d_recv.at[j], (role, dps[j], vocab))
    result = to_dp[0]
    for j in far[:-1]:
        arrived(from_dp.at[j], d_send.at[0], d_recv.at[j])
        result = result + from_dp[j]
    grad_ref[...] = result

    arrived(losses.at[1 - role], role_send.at[2], role_recv.at[2])
    both = losses[:, 0, :]
    loss_ref[...] = both
    mean_ref[...] = jnp.sum(jnp.sum(both, axis=1, keepdims=True), axis=0, keepdims=True) * (1.0 / rows)

    for copy in sent:
        copy.wait_send()

    @pl.loop(1, group)
    def _(step):
        stat_copy(step).wait_send()


def per_device(dp_size, vocab_size, teacher_hidden, student_hidden, teacher_unembed, student_unembed, targets):
    block_rows, t_depth = teacher_hidden.shape
    s_depth = student_hidden.shape[1]
    rows = dp_size * block_rows
    half = rows // 2
    cols = teacher_unembed.shape[1]
    group = dp_size * vocab_size
    f32, bf16 = jnp.float32, jnp.bfloat16
    vmem, dma = pltpu.VMEM, pltpu.SemaphoreType.DMA
    any_spec = pl.BlockSpec(memory_space=pl.ANY)
    vmem_spec = pl.BlockSpec(memory_space=pltpu.VMEM)
    losses, mean, grad = pl.pallas_call(
        functools.partial(kernel, dp_size, vocab_size),
        out_shape=(
            jax.ShapeDtypeStruct((2, half), f32),
            jax.ShapeDtypeStruct((1, 1), f32),
            jax.ShapeDtypeStruct((block_rows, s_depth), f32),
        ),
        in_specs=[any_spec] * 4 + [vmem_spec],
        out_specs=(vmem_spec,) * 3,
        scratch_shapes=[
            vmem((vocab_size, dp_size, block_rows, t_depth), bf16),
            vmem((vocab_size, dp_size, block_rows, s_depth), bf16),
            vmem(teacher_unembed.shape, bf16),
            vmem(student_unembed.shape, bf16),
            vmem((rows, cols), f32),
            vmem((rows, cols), f32),
            vmem((half, cols), f32),
            vmem((half, cols), f32),
            vmem((rows, LANES), jnp.int32),
            vmem((half, LANES), f32),
            vmem((group, 8, half), f32),
            vmem((2, 8, half), f32),
            vmem((half, LANES), f32),
            vmem((rows, cols), bf16),
            vmem((vocab_size, rows, s_depth), f32),
            vmem((vocab_size, rows, s_depth), f32),
            vmem((dp_size, block_rows, s_depth), f32),
            vmem((dp_size, block_rows, s_depth), f32),
            dma((4,)),
            dma((vocab_size, dp_size)),
            dma((vocab_size, dp_size)),
            dma((vocab_size, dp_size)),
            dma((vocab_size, dp_size)),
            dma((4,)),
            dma((4,)),
            dma((group,)),
            dma((group,)),
            dma((vocab_size, dp_size)),
            dma((vocab_size, dp_size)),
            dma((dp_size,)),
            dma((dp_size,)),
        ],
        compiler_params=pltpu.CompilerParams(
            collective_id=0, has_side_effects=True, vmem_limit_bytes=50 * 1024 * 1024
        ),
    )(teacher_hidden, student_hidden, teacher_unembed, student_unembed, targets.reshape(1, rows))
    return losses.reshape(rows), mean.reshape(()), grad


def solution(mesh):
    return jax.shard_map(
        functools.partial(per_device, mesh.shape["dp"], mesh.shape["vocab"]),
        mesh=mesh,
        in_specs=(
            P("dp", ("role", "vocab")),
            P("dp", ("role", "vocab")),
            P("role", ("dp", "vocab")),
            P("role", ("dp", "vocab")),
            P(),
        ),
        out_specs=(P(), P(), P("dp", ("role", "vocab"))),
        check_vma=False,
    )
```

```python
import functools

import jax
import jax.numpy as jnp
from jax import lax
from jax.experimental import pallas as pl
from jax.experimental.pallas import tpu as pltpu
from jax.sharding import PartitionSpec as P

MESH = pl.DeviceIdType.MESH
TILE = 256
ROW_STEP = 32
LANES = 128
HOP = jnp.float32


def flipped(index, bits, size):
    out, bit = index, 1
    while bit < size:
        if bits & bit:
            out = out + bit * (1 - 2 * lax.rem(lax.div(index, bit), 2))
        bit *= 2
    return out


def kernel(
    dp_size, vocab_size,
    th_ref, sh_ref, tw_ref, sw_ref, targets_ref,
    loss_ref, mean_ref, grad_ref,
    th, sh, tw, sw, targets, t_acc, s_acc, t_other, s_other, target_col, stat_col, stats, losses, lse_col,
    logit_grad, term, from_vocab, out_hop, in_hop, middle, in_last, to_dp, from_dp,
    local_sem, t_send, t_recv, s_send, s_recv, role_send, role_recv,
    stat_send, stat_recv, v_send, v_recv, h_send, h_recv, d_send, d_recv,
):
    role, dp, vocab = lax.axis_index("role"), lax.axis_index("dp"), lax.axis_index("vocab")
    group = dp_size * vocab_size
    me = dp * vocab_size + vocab
    cols = tw.shape[1]
    block_rows = th_ref.shape[0]
    rows = dp_size * block_rows
    half = rows // 2
    features = sh_ref.shape[1]
    dps = [flipped(dp, k, dp_size) for k in range(dp_size)]
    vocabs = [flipped(vocab, k, vocab_size) for k in range(vocab_size)]
    partner = (1 - role, dp, vocab)
    sent = []

    def send(src, dst, send_sem, recv_sem, device):
        copy = pltpu.make_async_remote_copy(
            src_ref=src, dst_ref=dst, send_sem=send_sem, recv_sem=recv_sem,
            device_id=device, device_id_type=MESH,
        )
        copy.start()
        sent.append(copy)

    def arrived(dst, send_sem, recv_sem):
        pltpu.make_async_remote_copy(
            src_ref=dst, dst_ref=dst, send_sem=send_sem, recv_sem=recv_sem,
            device_id=partner, device_id_type=MESH,
        ).wait_recv()

    tw_copy = pltpu.make_async_copy(tw_ref, tw, local_sem.at[0])
    sw_copy = pltpu.make_async_copy(sw_ref, sw, local_sem.at[1])
    th_copy = pltpu.make_async_copy(th_ref, th.at[vocab, dp], local_sem.at[2])
    sh_copy = pltpu.make_async_copy(sh_ref, sh.at[vocab, dp], local_sem.at[3])
    targets_copy = pltpu.make_async_copy(targets_ref, targets, local_sem.at[4])
    for copy in (th_copy, sh_copy, tw_copy, sw_copy, targets_copy):
        copy.start()

    barrier = pltpu.get_barrier_semaphore()

    neighbours = [(role, dps[k], vocab) for k in range(1, dp_size)]
    neighbours += [(role, dp, vocabs[k]) for k in range(1, vocab_size)]
    for neighbour in neighbours + [partner]:
        pl.semaphore_signal(barrier, inc=1, device_id=neighbour, device_id_type=MESH)
    pl.semaphore_wait(barrier, dp_size + vocab_size - 1)

    corner = vocab_size == 4
    direct = (1, 2) if corner else tuple(range(1, vocab_size))
    teacher_part = (th, t_send, t_recv)
    student_part = (sh, s_send, s_recv)
    for source, (held, send_sem, recv_sem) in ((th_ref, teacher_part), (sh_ref, student_part)):
        for k in range(1, dp_size):
            send(
                source, held.at[vocab, dp], send_sem.at[0, k], recv_sem.at[vocab, dp],
                (role, dps[k], vocab),
            )
        for k in direct:
            send(
                source, held.at[vocab, dp], send_sem.at[k, 0], recv_sem.at[vocab, dp],
                (role, dp, vocabs[k]),
            )

    targets_copy.wait()
    target_col[...] = jnp.transpose(jnp.broadcast_to(targets[...], (LANES, rows)))

    def pass_on(part, j):
        held, send_sem, recv_sem = part
        slot = held.at[vocab, dps[j]]
        arrived(slot, send_sem.at[0, 0], recv_sem.at[vocab, dps[j]])
        for k in direct:
            send(
                slot, slot, send_sem.at[k, j], recv_sem.at[vocab, dps[j]],
                (role, dp, vocabs[k]),
            )

    def relay(part, j):
        if not corner:
            return
        held, send_sem, recv_sem = part
        middle = block_rows // 2
        for k, at in ((1, pl.ds(0, middle)), (2, pl.ds(middle, middle))):
            slot = (vocabs[k], dps[j])
            arrived(held.at[slot], send_sem.at[0, 0], recv_sem.at[slot])
            piece = held.at[slot[0], slot[1], at]
            send(
                piece, piece, send_sem.at[vocab_size + k - 1, j], recv_sem.at[slot],
                (role, dp, vocabs[3 - k]),
            )

    def add_product(held, weights, acc, k):
        depth = held.shape[-1]
        start = pl.multiple_of(vocabs[k] * depth, 16)

        @pl.loop(0, cols // TILE)
        def _(n):
            at = pl.ds(pl.multiple_of(n * TILE, TILE), TILE)
            product = jnp.dot(
                held[vocabs[k]].reshape(rows, depth),
                weights[pl.ds(start, depth), at],
                preferred_element_type=jnp.float32,
            )
            if k == 0:
                acc[:, at] = product
            else:
                acc[:, at] += product

    def add_arriving(part, weights, acc, ks):
        held, send_sem, recv_sem = part
        for k in ks:
            if k == 3 or not corner:
                for j in range(dp_size):
                    slot = (vocabs[k], dps[j])
                    arrived(held.at[slot], send_sem.at[0, 0], recv_sem.at[slot])
            add_product(held, weights, acc, k)

    own_rows = pl.multiple_of(role * half, ROW_STEP)
    other_rows = pl.multiple_of((1 - role) * half, ROW_STEP)

    for j in range(1, dp_size):
        pass_on(teacher_part, j)
    th_copy.wait()
    tw_copy.wait()
    add_product(th, tw, t_acc, 0)
    relay(teacher_part, 0)
    for j in range(1, dp_size):
        relay(teacher_part, j)
        pass_on(student_part, j)
    sh_copy.wait()
    sw_copy.wait()
    for j in range(dp_size):
        relay(student_part, j)
    add_product(sh, sw, s_acc, 0)
    early, late = ((1, 2), (3,)) if corner else ((), direct)
    add_arriving(teacher_part, tw, t_acc, early)
    add_arriving(student_part, sw, s_acc, early)
    add_arriving(teacher_part, tw, t_acc, late)
    send(t_acc.at[pl.ds(other_rows, half)], t_other, role_send.at[0], role_recv.at[0], partner)
    add_arriving(student_part, sw, s_acc, late)
    send(s_acc.at[pl.ds(other_rows, half)], s_other, role_send.at[1], role_recv.at[1], partner)
    arrived(t_other, role_send.at[0], role_recv.at[0])
    arrived(s_other, role_send.at[1], role_recv.at[1])

    column = lax.broadcasted_iota(jnp.int32, (ROW_STEP, cols), 1) + me * cols
    lane = lax.broadcasted_iota(jnp.int32, (ROW_STEP, LANES), 1)

    def at_rows(step):
        local = pl.ds(pl.multiple_of(step * ROW_STEP, ROW_STEP), ROW_STEP)
        whole = pl.ds(pl.multiple_of(own_rows + step * ROW_STEP, ROW_STEP), ROW_STEP)
        return local, whole

    @pl.loop(0, half // ROW_STEP)
    def _(step):
        local, whole = at_rows(step)
        teacher = t_acc[whole, :] + t_other[local, :]
        student = s_acc[whole, :] + s_other[local, :]
        hit = column == target_col[whole, 0:1]
        t_top = jnp.max(teacher, axis=1, keepdims=True)
        s_top = jnp.max(student, axis=1, keepdims=True)
        t_exp = jnp.exp(teacher - t_top)
        t_sum = jnp.sum(t_exp, axis=1, keepdims=True)
        gap = jnp.sum(t_exp * (teacher - student), axis=1, keepdims=True)
        s_sum = jnp.sum(jnp.exp(student - s_top), axis=1, keepdims=True)
        label = jnp.sum(jnp.where(hit, student, 0.0), axis=1, keepdims=True)
        packed = jnp.zeros((ROW_STEP, LANES), jnp.float32)
        for place, value in enumerate((t_top, t_sum, gap, s_top, s_sum, label)):
            packed = jnp.where(lane == place, value, packed)
        stat_col[local, :] = packed

    stats[me] = jnp.transpose(stat_col[...])[0:8, :]

    def stat_copy(step):
        other = lax.rem(me + step, group)
        return pltpu.make_async_remote_copy(
            src_ref=stats.at[me], dst_ref=stats.at[me],
            send_sem=stat_send.at[step], recv_sem=stat_recv.at[me],
            device_id=(role, lax.div(other, vocab_size), lax.rem(other, vocab_size)),
            device_id_type=MESH,
        )

    @pl.loop(1, group)
    def _(step):
        stat_copy(step).start()

    @pl.loop(1, group)
    def _(step):
        other = lax.rem(me + step, group)
        arrived(stats.at[other], stat_send.at[0], stat_recv.at[other])

    everyone = stats[...]
    t_top, t_sum, gap = everyone[:, 0, :], everyone[:, 1, :], everyone[:, 2, :]
    s_top, s_sum, label = everyone[:, 3, :], everyone[:, 4, :], everyone[:, 5, :]
    t_max = jnp.max(t_top, axis=0, keepdims=True)
    s_max = jnp.max(s_top, axis=0, keepdims=True)
    t_scale = jnp.exp(t_top - t_max)
    t_total = jnp.sum(t_sum * t_scale, axis=0, keepdims=True)
    s_total = jnp.sum(s_sum * jnp.exp(s_top - s_max), axis=0, keepdims=True)
    t_lse = t_max + jnp.log(t_total)
    s_lse = s_max + jnp.log(s_total)
    mean_gap = jnp.sum(gap * t_scale, axis=0, keepdims=True) / t_total
    s_label = jnp.sum(label, axis=0, keepdims=True)
    loss = (mean_gap - t_lse + s_lse) - (s_label - s_lse)
    losses[role] = jnp.broadcast_to(loss, (8, half))
    send(losses.at[role], losses.at[role], role_send.at[2], role_recv.at[2], partner)
    first = lax.broadcasted_iota(jnp.int32, (LANES, half), 0) == 0
    lse_col[...] = jnp.transpose(jnp.where(first, t_lse, s_lse))

    @pl.loop(0, half // ROW_STEP)
    def _(step):
        local, whole = at_rows(step)
        teacher = t_acc[whole, :] + t_other[local, :]
        student = s_acc[whole, :] + s_other[local, :]
        onehot = jnp.where(column == target_col[whole, 0:1], 1.0, 0.0)
        t_prob = jnp.exp(teacher - lse_col[local, 0:1])
        s_prob = jnp.exp(student - lse_col[local, 1:2])
        logit_grad[whole, :] = (2.0 * s_prob - t_prob - onehot).astype(jnp.bfloat16)

    mine = logit_grad.at[pl.ds(own_rows, half)]
    send(mine, mine, role_send.at[3], role_recv.at[3], partner)
    arrived(logit_grad.at[pl.ds(other_rows, half)], role_send.at[3], role_recv.at[3])

    def block(j):
        return pl.ds(pl.multiple_of(dps[j] * block_rows, block_rows), block_rows)

    def send_term(k, j):
        send(
            term.at[k, block(j)], from_vocab.at[k, block(j)],
            v_send.at[k, j], v_recv.at[k, dps[j]], (role, dp, vocabs[k]),
        )

    far = list(range(dp_size - 1, -1, -1))

    def product(k, n, width):
        start = pl.multiple_of(vocabs[k] * features + n * width, width)
        return lax.dot_general(
            logit_grad[...], sw[pl.ds(start, width), :],
            (((1,), (1,)), ((), ())), preferred_element_type=jnp.float32,
        )

    def finish(j, total):
        to_dp[j] = total
        if j:
            send(to_dp.at[j], from_dp.at[j], d_send.at[j], d_recv.at[j], (role, dps[j], vocab))

    if corner:
        width = features // 2
        sides = (pl.ds(0, width), pl.ds(width, width))

        def hop(side, slot, j):
            send(
                out_hop.at[side, slot, block(j)], in_hop.at[side, slot, block(j)],
                h_send.at[side, slot, j], h_recv.at[side, slot, dps[j]],
                (role, dp, vocabs[1 + side]),
            )

        def landed(buffer, side, slot, j):
            arrived(
                buffer.at[side, slot, block(j)] if slot < 2 else buffer.at[side, block(j)],
                h_send.at[0, 0, 0], h_recv.at[side, slot, dps[j]],
            )

        for side in (0, 1):
            out_hop[side, 1] = product(3, side, width).astype(HOP)
            for j in far:
                hop(side, 1, j)
        for side in (0, 1):
            out_hop[side, 0] = product(1 + side, side, width).astype(HOP)
            hop(side, 0, far[0])
        for side in (0, 1):
            middle[side] = product(2 - side, side, width)
        for side in (0, 1):
            term[0, :, sides[side]] = product(0, side, width)
        for at, j in enumerate(far):
            for side in (0, 1):
                landed(in_hop, side, 1, j)
                middle[side, block(j)] += in_hop[side, 1, block(j)].astype(jnp.float32)
                send(
                    middle.at[side, block(j)], in_last.at[side, block(j)],
                    h_send.at[side, 2, j], h_recv.at[side, 2, dps[j]],
                    (role, dp, vocabs[2 - side]),
                )
            if at + 1 < dp_size:
                for side in (0, 1):
                    hop(side, 0, far[at + 1])
        for j in far:
            totals = []
            for side in (0, 1):
                landed(in_hop, side, 0, j)
                near = term[0, block(j), sides[side]] + in_hop[side, 0, block(j)].astype(jnp.float32)
                landed(in_last, side, 2, j)
                totals.append(near + in_last[side, block(j)])
            finish(j, jnp.concatenate(totals, axis=1))
    else:
        width = min(TILE, features)
        order = list(range(vocab_size - 1, -1, -1))
        for k in order:
            @pl.loop(0, features // width)
            def _(n):
                term[k, :, pl.ds(pl.multiple_of(n * width, width), width)] = product(k, n, width)
            if k:
                send_term(k, far[0])
        for j in far[1:]:
            for k in order[:-1]:
                send_term(k, j)
        for j in far:
            total = term[0, block(j), :]
            for k in order[:-1]:
                arrived(from_vocab.at[k, block(j)], v_send.at[0, 0], v_recv.at[k, dps[j]])
                total = total + from_vocab[k, block(j), :]
            finish(j, total)
    result = to_dp[0]
    for j in far[:-1]:
        arrived(from_dp.at[j], d_send.at[0], d_recv.at[j])
        result = result + from_dp[j]
    grad_ref[...] = result

    arrived(losses.at[1 - role], role_send.at[2], role_recv.at[2])
    both = losses[:, 0, :]
    loss_ref[...] = both
    mean_ref[...] = jnp.sum(jnp.sum(both, axis=1, keepdims=True), axis=0, keepdims=True) * (1.0 / rows)

    for copy in sent:
        copy.wait_send()

    @pl.loop(1, group)
    def _(step):
        stat_copy(step).wait_send()


def per_device(dp_size, vocab_size, teacher_hidden, student_hidden, teacher_unembed, student_unembed, targets):
    block_rows, t_depth = teacher_hidden.shape
    s_depth = student_hidden.shape[1]
    rows = dp_size * block_rows
    half = rows // 2
    cols = teacher_unembed.shape[1]
    group = dp_size * vocab_size
    corner = vocab_size == 4
    hop_rows = rows if corner else 16
    f32, bf16 = jnp.float32, jnp.bfloat16
    vmem, dma = pltpu.VMEM, pltpu.SemaphoreType.DMA
    any_spec = pl.BlockSpec(memory_space=pltpu.HBM)
    vmem_spec = pl.BlockSpec(memory_space=pltpu.VMEM)
    losses, mean, grad = pl.pallas_call(
        functools.partial(kernel, dp_size, vocab_size),
        out_shape=(
            jax.ShapeDtypeStruct((2, half), f32),
            jax.ShapeDtypeStruct((1, 1), f32),
            jax.ShapeDtypeStruct((block_rows, s_depth), f32),
        ),
        in_specs=[any_spec] * 5,
        out_specs=(vmem_spec,) * 3,
        scratch_shapes=[
            vmem((vocab_size, dp_size, block_rows, t_depth), bf16),
            vmem((vocab_size, dp_size, block_rows, s_depth), bf16),
            vmem(teacher_unembed.shape, bf16),
            vmem(student_unembed.shape, bf16),
            vmem((1, rows), jnp.int32),
            vmem((rows, cols), f32),
            vmem((rows, cols), f32),
            vmem((half, cols), f32),
            vmem((half, cols), f32),
            vmem((rows, LANES), jnp.int32),
            vmem((half, LANES), f32),
            vmem((group, 8, half), f32),
            vmem((2, 8, half), f32),
            vmem((half, LANES), f32),
            vmem((rows, cols), bf16),
            vmem((1 if corner else vocab_size, rows, s_depth), f32),
            vmem((1 if corner else vocab_size, 8 if corner else rows, s_depth), f32),
            vmem((2, 2, hop_rows, s_depth // 2), HOP),
            vmem((2, 2, hop_rows, s_depth // 2), HOP),
            vmem((2, hop_rows, s_depth // 2), f32),
            vmem((2, hop_rows, s_depth // 2), f32),
            vmem((dp_size, block_rows, s_depth), f32),
            vmem((dp_size, block_rows, s_depth), f32),
            dma((5,)),
            dma((vocab_size + 2, dp_size)),
            dma((vocab_size, dp_size)),
            dma((vocab_size + 2, dp_size)),
            dma((vocab_size, dp_size)),
            dma((4,)),
            dma((4,)),
            dma((group,)),
            dma((group,)),
            dma((vocab_size, dp_size)),
            dma((vocab_size, dp_size)),
            dma((2, 3, dp_size)),
            dma((2, 3, dp_size)),
            dma((dp_size,)),
            dma((dp_size,)),
        ],
        compiler_params=pltpu.CompilerParams(
            collective_id=0, has_side_effects=True, vmem_limit_bytes=50 * 1024 * 1024
        ),
    )(teacher_hidden, student_hidden, teacher_unembed, student_unembed, targets.reshape(1, rows))
    return losses.reshape(rows), mean.reshape(()), grad


def solution(mesh):
    return jax.shard_map(
        functools.partial(per_device, mesh.shape["dp"], mesh.shape["vocab"]),
        mesh=mesh,
        in_specs=(
            P("dp", ("role", "vocab")),
            P("dp", ("role", "vocab")),
            P("role", ("dp", "vocab")),
            P("role", ("dp", "vocab")),
            P(),
        ),
        out_specs=(P(), P(), P("dp", ("role", "vocab"))),
        check_vma=False,
    )
```

```python
import functools

import jax
import jax.numpy as jnp
from jax import lax
from jax.experimental import pallas as pl
from jax.experimental.pallas import tpu as pltpu
from jax.sharding import PartitionSpec as P

MESH = pl.DeviceIdType.MESH
TILE = 256
ROW_STEP = 32
LANES = 128
HOP = jnp.float32


def flipped(index, bits, size):
    out, bit = index, 1
    while bit < size:
        if bits & bit:
            out = out + bit * (1 - 2 * lax.rem(lax.div(index, bit), 2))
        bit *= 2
    return out


def kernel(
    dp_size, vocab_size,
    th_ref, sh_ref, tw_ref, sw_ref, targets_ref,
    loss_ref, mean_ref, grad_ref,
    th, sh, tw, sw, targets, t_acc, s_acc, t_other, s_other, target_col, stat_col, stats, losses, lse_col,
    logit_grad, term, from_vocab, out_hop, in_hop, middle, in_last, to_dp, from_dp,
    local_sem, t_send, t_recv, s_send, s_recv, role_send, role_recv,
    stat_send, stat_recv, v_send, v_recv, h_send, h_recv, d_send, d_recv,
):
    role, dp, vocab = lax.axis_index("role"), lax.axis_index("dp"), lax.axis_index("vocab")
    group = dp_size * vocab_size
    me = dp * vocab_size + vocab
    cols = tw.shape[1]
    block_rows = th_ref.shape[0]
    rows = dp_size * block_rows
    half = rows // 2
    features = sh_ref.shape[1]
    dps = [flipped(dp, k, dp_size) for k in range(dp_size)]
    vocabs = [flipped(vocab, k, vocab_size) for k in range(vocab_size)]
    partner = (1 - role, dp, vocab)
    sent = []

    def send(src, dst, send_sem, recv_sem, device):
        copy = pltpu.make_async_remote_copy(
            src_ref=src, dst_ref=dst, send_sem=send_sem, recv_sem=recv_sem,
            device_id=device, device_id_type=MESH,
        )
        copy.start()
        sent.append(copy)

    def arrived(dst, send_sem, recv_sem):
        pltpu.make_async_remote_copy(
            src_ref=dst, dst_ref=dst, send_sem=send_sem, recv_sem=recv_sem,
            device_id=partner, device_id_type=MESH,
        ).wait_recv()

    tw_copy = pltpu.make_async_copy(tw_ref, tw, local_sem.at[0])
    sw_copy = pltpu.make_async_copy(sw_ref, sw, local_sem.at[1])
    th_copy = pltpu.make_async_copy(th_ref, th.at[vocab, dp], local_sem.at[2])
    sh_copy = pltpu.make_async_copy(sh_ref, sh.at[vocab, dp], local_sem.at[3])
    targets_copy = pltpu.make_async_copy(targets_ref, targets, local_sem.at[4])
    for copy in (th_copy, sh_copy, tw_copy, sw_copy, targets_copy):
        copy.start()

    barrier = pltpu.get_barrier_semaphore()

    neighbours = [(role, dps[k], vocab) for k in range(1, dp_size)]
    neighbours += [(role, dp, vocabs[k]) for k in range(1, vocab_size)]
    for neighbour in neighbours + [partner]:
        pl.semaphore_signal(barrier, inc=1, device_id=neighbour, device_id_type=MESH)
    pl.semaphore_wait(barrier, dp_size + vocab_size - 1)

    corner = vocab_size == 4
    direct = (1, 2) if corner else tuple(range(1, vocab_size))
    teacher_part = (th, t_send, t_recv)
    student_part = (sh, s_send, s_recv)
    for source, (held, send_sem, recv_sem) in ((th_ref, teacher_part), (sh_ref, student_part)):
        for k in range(1, dp_size):
            send(
                source, held.at[vocab, dp], send_sem.at[0, k], recv_sem.at[vocab, dp],
                (role, dps[k], vocab),
            )
        for k in direct:
            send(
                source, held.at[vocab, dp], send_sem.at[k, 0], recv_sem.at[vocab, dp],
                (role, dp, vocabs[k]),
            )

    targets_copy.wait()
    target_col[...] = jnp.transpose(jnp.broadcast_to(targets[...], (LANES, rows)))

    def pass_on(part, j):
        held, send_sem, recv_sem = part
        slot = held.at[vocab, dps[j]]
        arrived(slot, send_sem.at[0, 0], recv_sem.at[vocab, dps[j]])
        for k in direct:
            send(
                slot, slot, send_sem.at[k, j], recv_sem.at[vocab, dps[j]],
                (role, dp, vocabs[k]),
            )

    def relay(part, j):
        if not corner:
            return
        held, send_sem, recv_sem = part
        middle = block_rows // 2
        for k, at in ((1, pl.ds(0, middle)), (2, pl.ds(middle, middle))):
            slot = (vocabs[k], dps[j])
            arrived(held.at[slot], send_sem.at[0, 0], recv_sem.at[slot])
            piece = held.at[slot[0], slot[1], at]
            send(
                piece, piece, send_sem.at[vocab_size + k - 1, j], recv_sem.at[slot],
                (role, dp, vocabs[3 - k]),
            )

    def add_product(held, weights, acc, k):
        depth = held.shape[-1]
        start = pl.multiple_of(vocabs[k] * depth, 16)

        @pl.loop(0, cols // TILE)
        def _(n):
            at = pl.ds(pl.multiple_of(n * TILE, TILE), TILE)
            product = jnp.dot(
                held[vocabs[k]].reshape(rows, depth),
                weights[pl.ds(start, depth), at],
                preferred_element_type=jnp.float32,
            )
            if k == 0:
                acc[:, at] = product
            else:
                acc[:, at] += product

    def add_arriving(part, weights, acc, ks):
        held, send_sem, recv_sem = part
        for k in ks:
            if k == 3 or not corner:
                for j in range(dp_size):
                    slot = (vocabs[k], dps[j])
                    arrived(held.at[slot], send_sem.at[0, 0], recv_sem.at[slot])
            add_product(held, weights, acc, k)

    own_rows = pl.multiple_of(role * half, ROW_STEP)
    other_rows = pl.multiple_of((1 - role) * half, ROW_STEP)

    early, late = ((1, 2), (3,)) if corner else ((), direct)
    pass_on(teacher_part, 1)
    relay(teacher_part, 0)
    for j in range(2, dp_size):
        pass_on(teacher_part, j)
    relay(student_part, 0)
    pass_on(student_part, 1)
    for j in range(1, dp_size):
        relay(teacher_part, j)
        if j + 1 < dp_size:
            pass_on(student_part, j + 1)
    th_copy.wait()
    tw_copy.wait()
    add_product(th, tw, t_acc, 0)
    for j in range(1, dp_size):
        relay(student_part, j)
    sh_copy.wait()
    sw_copy.wait()
    add_arriving(teacher_part, tw, t_acc, early)
    add_product(sh, sw, s_acc, 0)
    add_arriving(student_part, sw, s_acc, early)
    add_arriving(teacher_part, tw, t_acc, late)
    send(t_acc.at[pl.ds(other_rows, half)], t_other, role_send.at[0], role_recv.at[0], partner)
    add_arriving(student_part, sw, s_acc, late)
    send(s_acc.at[pl.ds(other_rows, half)], s_other, role_send.at[1], role_recv.at[1], partner)
    arrived(t_other, role_send.at[0], role_recv.at[0])
    arrived(s_other, role_send.at[1], role_recv.at[1])

    column = lax.broadcasted_iota(jnp.int32, (ROW_STEP, cols), 1) + me * cols
    lane = lax.broadcasted_iota(jnp.int32, (ROW_STEP, LANES), 1)

    def at_rows(step):
        local = pl.ds(pl.multiple_of(step * ROW_STEP, ROW_STEP), ROW_STEP)
        whole = pl.ds(pl.multiple_of(own_rows + step * ROW_STEP, ROW_STEP), ROW_STEP)
        return local, whole

    @pl.loop(0, half // ROW_STEP)
    def _(step):
        local, whole = at_rows(step)
        teacher = t_acc[whole, :] + t_other[local, :]
        student = s_acc[whole, :] + s_other[local, :]
        hit = column == target_col[whole, 0:1]
        t_top = jnp.max(teacher, axis=1, keepdims=True)
        s_top = jnp.max(student, axis=1, keepdims=True)
        t_exp = jnp.exp(teacher - t_top)
        t_sum = jnp.sum(t_exp, axis=1, keepdims=True)
        gap = jnp.sum(t_exp * (teacher - student), axis=1, keepdims=True)
        s_sum = jnp.sum(jnp.exp(student - s_top), axis=1, keepdims=True)
        label = jnp.sum(jnp.where(hit, student, 0.0), axis=1, keepdims=True)
        packed = jnp.zeros((ROW_STEP, LANES), jnp.float32)
        for place, value in enumerate((t_top, t_sum, gap, s_top, s_sum, label)):
            packed = jnp.where(lane == place, value, packed)
        stat_col[local, :] = packed

    stats[me] = jnp.transpose(stat_col[...])[0:8, :]

    def stat_copy(step):
        other = lax.rem(me + step, group)
        return pltpu.make_async_remote_copy(
            src_ref=stats.at[me], dst_ref=stats.at[me],
            send_sem=stat_send.at[step], recv_sem=stat_recv.at[me],
            device_id=(role, lax.div(other, vocab_size), lax.rem(other, vocab_size)),
            device_id_type=MESH,
        )

    @pl.loop(1, group)
    def _(step):
        stat_copy(step).start()

    @pl.loop(1, group)
    def _(step):
        other = lax.rem(me + step, group)
        arrived(stats.at[other], stat_send.at[0], stat_recv.at[other])

    everyone = stats[...]
    t_top, t_sum, gap = everyone[:, 0, :], everyone[:, 1, :], everyone[:, 2, :]
    s_top, s_sum, label = everyone[:, 3, :], everyone[:, 4, :], everyone[:, 5, :]
    t_max = jnp.max(t_top, axis=0, keepdims=True)
    s_max = jnp.max(s_top, axis=0, keepdims=True)
    t_scale = jnp.exp(t_top - t_max)
    t_total = jnp.sum(t_sum * t_scale, axis=0, keepdims=True)
    s_total = jnp.sum(s_sum * jnp.exp(s_top - s_max), axis=0, keepdims=True)
    t_lse = t_max + jnp.log(t_total)
    s_lse = s_max + jnp.log(s_total)
    mean_gap = jnp.sum(gap * t_scale, axis=0, keepdims=True) / t_total
    s_label = jnp.sum(label, axis=0, keepdims=True)
    loss = (mean_gap - t_lse + s_lse) - (s_label - s_lse)
    losses[role] = jnp.broadcast_to(loss, (8, half))
    send(losses.at[role], losses.at[role], role_send.at[2], role_recv.at[2], partner)
    first = lax.broadcasted_iota(jnp.int32, (LANES, half), 0) == 0
    lse_col[...] = jnp.transpose(jnp.where(first, t_lse, s_lse))

    @pl.loop(0, half // ROW_STEP)
    def _(step):
        local, whole = at_rows(step)
        teacher = t_acc[whole, :] + t_other[local, :]
        student = s_acc[whole, :] + s_other[local, :]
        onehot = jnp.where(column == target_col[whole, 0:1], 1.0, 0.0)
        t_prob = jnp.exp(teacher - lse_col[local, 0:1])
        s_prob = jnp.exp(student - lse_col[local, 1:2])
        logit_grad[whole, :] = (2.0 * s_prob - t_prob - onehot).astype(jnp.bfloat16)

    mine = logit_grad.at[pl.ds(own_rows, half)]
    send(mine, mine, role_send.at[3], role_recv.at[3], partner)
    arrived(logit_grad.at[pl.ds(other_rows, half)], role_send.at[3], role_recv.at[3])

    def block(j):
        return pl.ds(pl.multiple_of(dps[j] * block_rows, block_rows), block_rows)

    def send_term(k, j):
        send(
            term.at[k, block(j)], from_vocab.at[k, block(j)],
            v_send.at[k, j], v_recv.at[k, dps[j]], (role, dp, vocabs[k]),
        )

    far = list(range(dp_size - 1, -1, -1))

    def product(k, n, width):
        start = pl.multiple_of(vocabs[k] * features + n * width, width)
        return lax.dot_general(
            logit_grad[...], sw[pl.ds(start, width), :],
            (((1,), (1,)), ((), ())), preferred_element_type=jnp.float32,
        )

    def finish(j, total):
        to_dp[j] = total
        if j:
            send(to_dp.at[j], from_dp.at[j], d_send.at[j], d_recv.at[j], (role, dps[j], vocab))

    if corner:
        width = features // 2
        sides = (pl.ds(0, width), pl.ds(width, width))

        def hop(side, slot, j):
            send(
                out_hop.at[side, slot, block(j)], in_hop.at[side, slot, block(j)],
                h_send.at[side, slot, j], h_recv.at[side, slot, dps[j]],
                (role, dp, vocabs[1 + side]),
            )

        def landed(buffer, side, slot, j):
            arrived(
                buffer.at[side, slot, block(j)] if slot < 2 else buffer.at[side, block(j)],
                h_send.at[0, 0, 0], h_recv.at[side, slot, dps[j]],
            )

        def sum_middle(j):
            for side in (0, 1):
                landed(in_hop, side, 1, j)
                middle[side, block(j)] += in_hop[side, 1, block(j)].astype(jnp.float32)
                send(
                    middle.at[side, block(j)], in_last.at[side, block(j)],
                    h_send.at[side, 2, j], h_recv.at[side, 2, dps[j]],
                    (role, dp, vocabs[2 - side]),
                )

        def sum_last(j):
            totals = []
            for side in (0, 1):
                landed(in_hop, side, 0, j)
                near = term[0, block(j), sides[side]] + in_hop[side, 0, block(j)].astype(jnp.float32)
                landed(in_last, side, 2, j)
                totals.append(near + in_last[side, block(j)])
            finish(j, jnp.concatenate(totals, axis=1))

        for side in (0, 1):
            out_hop[side, 1] = product(3, side, width).astype(HOP)
            hop(side, 1, far[0])
        for side in (0, 1):
            out_hop[side, 0] = product(1 + side, side, width).astype(HOP)
            hop(side, 0, far[0])
            for j in far[1:2]:
                hop(side, 1, j)
        for side in (0, 1):
            middle[side] = product(2 - side, side, width)
        for side in (0, 1):
            term[0, :, sides[side]] = product(0, side, width)
        for at, j in enumerate(far):
            sum_middle(j)
            for side in (0, 1):
                for later in far[at + 1:at + 2]:
                    hop(side, 0, later)
                for later in far[at + 2:at + 3]:
                    hop(side, 1, later)
            if at:
                sum_last(far[at - 1])
        sum_last(far[-1])
    else:
        width = min(TILE, features)
        order = list(range(vocab_size - 1, -1, -1))
        for k in order:
            @pl.loop(0, features // width)
            def _(n):
                term[k, :, pl.ds(pl.multiple_of(n * width, width), width)] = product(k, n, width)
            if k:
                send_term(k, far[0])
        for j in far[1:]:
            for k in order[:-1]:
                send_term(k, j)
        for j in far:
            total = term[0, block(j), :]
            for k in order[:-1]:
                arrived(from_vocab.at[k, block(j)], v_send.at[0, 0], v_recv.at[k, dps[j]])
                total = total + from_vocab[k, block(j), :]
            finish(j, total)
    result = to_dp[0]
    for j in far[:-1]:
        arrived(from_dp.at[j], d_send.at[0], d_recv.at[j])
        result = result + from_dp[j]
    grad_ref[...] = result

    arrived(losses.at[1 - role], role_send.at[2], role_recv.at[2])
    both = losses[:, 0, :]
    loss_ref[:, 0:half] = both[0:1]
    loss_ref[:, half:rows] = both[1:2]
    mean_ref[...] = jnp.sum(jnp.sum(both, axis=1, keepdims=True), axis=0, keepdims=True) * (1.0 / rows)

    for copy in sent:
        copy.wait_send()

    @pl.loop(1, group)
    def _(step):
        stat_copy(step).wait_send()


def per_device(dp_size, vocab_size, teacher_hidden, student_hidden, teacher_unembed, student_unembed, targets):
    block_rows, t_depth = teacher_hidden.shape
    s_depth = student_hidden.shape[1]
    rows = dp_size * block_rows
    half = rows // 2
    cols = teacher_unembed.shape[1]
    group = dp_size * vocab_size
    corner = vocab_size == 4
    hop_rows = rows if corner else 16
    f32, bf16 = jnp.float32, jnp.bfloat16
    vmem, dma = pltpu.VMEM, pltpu.SemaphoreType.DMA
    any_spec = pl.BlockSpec(memory_space=pltpu.HBM)
    vmem_spec = pl.BlockSpec(memory_space=pltpu.VMEM)
    losses, mean, grad = pl.pallas_call(
        functools.partial(kernel, dp_size, vocab_size),
        out_shape=(
            jax.ShapeDtypeStruct((1, rows), f32),
            jax.ShapeDtypeStruct((1, 1), f32),
            jax.ShapeDtypeStruct((block_rows, s_depth), f32),
        ),
        in_specs=[any_spec] * 5,
        out_specs=(vmem_spec,) * 3,
        scratch_shapes=[
            vmem((vocab_size, dp_size, block_rows, t_depth), bf16),
            vmem((vocab_size, dp_size, block_rows, s_depth), bf16),
            vmem(teacher_unembed.shape, bf16),
            vmem(student_unembed.shape, bf16),
            vmem((1, rows), jnp.int32),
            vmem((rows, cols), f32),
            vmem((rows, cols), f32),
            vmem((half, cols), f32),
            vmem((half, cols), f32),
            vmem((rows, LANES), jnp.int32),
            vmem((half, LANES), f32),
            vmem((group, 8, half), f32),
            vmem((2, 8, half), f32),
            vmem((half, LANES), f32),
            vmem((rows, cols), bf16),
            vmem((1 if corner else vocab_size, rows, s_depth), f32),
            vmem((1 if corner else vocab_size, 8 if corner else rows, s_depth), f32),
            vmem((2, 2, hop_rows, s_depth // 2), HOP),
            vmem((2, 2, hop_rows, s_depth // 2), HOP),
            vmem((2, hop_rows, s_depth // 2), f32),
            vmem((2, hop_rows, s_depth // 2), f32),
            vmem((dp_size, block_rows, s_depth), f32),
            vmem((dp_size, block_rows, s_depth), f32),
            dma((5,)),
            dma((vocab_size + 2, dp_size)),
            dma((vocab_size, dp_size)),
            dma((vocab_size + 2, dp_size)),
            dma((vocab_size, dp_size)),
            dma((4,)),
            dma((4,)),
            dma((group,)),
            dma((group,)),
            dma((vocab_size, dp_size)),
            dma((vocab_size, dp_size)),
            dma((2, 3, dp_size)),
            dma((2, 3, dp_size)),
            dma((dp_size,)),
            dma((dp_size,)),
        ],
        compiler_params=pltpu.CompilerParams(
            collective_id=0, has_side_effects=True, vmem_limit_bytes=50 * 1024 * 1024
        ),
    )(teacher_hidden, student_hidden, teacher_unembed, student_unembed, targets.reshape(1, rows))
    return losses.reshape(rows), mean.reshape(()), grad


def solution(mesh):
    return jax.shard_map(
        functools.partial(per_device, mesh.shape["dp"], mesh.shape["vocab"]),
        mesh=mesh,
        in_specs=(
            P("dp", ("role", "vocab")),
            P("dp", ("role", "vocab")),
            P("role", ("dp", "vocab")),
            P("role", ("dp", "vocab")),
            P(),
        ),
        out_specs=(P(), P(), P("dp", ("role", "vocab"))),
        check_vma=False,
    )
```

```python
import functools

import jax
import jax.numpy as jnp
from jax import lax
from jax.experimental import pallas as pl
from jax.experimental.pallas import tpu as pltpu
from jax.sharding import PartitionSpec as P

MESH = pl.DeviceIdType.MESH
TILE = 256
ROW_STEP = 32
LANES = 128
HOP = jnp.float32


def flipped(index, bits, size):
    out, bit = index, 1
    while bit < size:
        if bits & bit:
            out = out + bit * (1 - 2 * lax.rem(lax.div(index, bit), 2))
        bit *= 2
    return out


def kernel(
    dp_size, vocab_size,
    th_ref, sh_ref, tw_ref, sw_ref, targets_ref,
    loss_ref, mean_ref, grad_ref,
    th, sh, tw, sw, targets, t_acc, s_acc, t_other, s_other, target_col, stat_col, stats, losses, lse_col,
    logit_grad, term, from_vocab, out_hop, in_hop, middle, in_last, to_dp, from_dp,
    local_sem, t_send, t_recv, s_send, s_recv, role_send, role_recv,
    stat_send, stat_recv, v_send, v_recv, h_send, h_recv, d_send, d_recv,
):
    role, dp, vocab = lax.axis_index("role"), lax.axis_index("dp"), lax.axis_index("vocab")
    group = dp_size * vocab_size
    me = dp * vocab_size + vocab
    cols = tw.shape[1]
    block_rows = th_ref.shape[0]
    rows = dp_size * block_rows
    half = rows // 2
    features = sh_ref.shape[1]
    dps = [flipped(dp, k, dp_size) for k in range(dp_size)]
    vocabs = [flipped(vocab, k, vocab_size) for k in range(vocab_size)]
    partner = (1 - role, dp, vocab)
    sent = []

    def send(src, dst, send_sem, recv_sem, device):
        copy = pltpu.make_async_remote_copy(
            src_ref=src, dst_ref=dst, send_sem=send_sem, recv_sem=recv_sem,
            device_id=device, device_id_type=MESH,
        )
        copy.start()
        sent.append(copy)

    def arrived(dst, send_sem, recv_sem):
        pltpu.make_async_remote_copy(
            src_ref=dst, dst_ref=dst, send_sem=send_sem, recv_sem=recv_sem,
            device_id=partner, device_id_type=MESH,
        ).wait_recv()

    tw_copy = pltpu.make_async_copy(tw_ref, tw, local_sem.at[0])
    sw_copy = pltpu.make_async_copy(sw_ref, sw, local_sem.at[1])
    th_copy = pltpu.make_async_copy(th_ref, th.at[vocab, dp], local_sem.at[2])
    sh_copy = pltpu.make_async_copy(sh_ref, sh.at[vocab, dp], local_sem.at[3])
    targets_copy = pltpu.make_async_copy(targets_ref, targets, local_sem.at[4])
    for copy in (th_copy, sh_copy, tw_copy, sw_copy, targets_copy):
        copy.start()

    barrier = pltpu.get_barrier_semaphore()

    neighbours = [(role, dps[k], vocab) for k in range(1, dp_size)]
    neighbours += [(role, dp, vocabs[k]) for k in range(1, vocab_size)]
    for neighbour in neighbours + [partner]:
        pl.semaphore_signal(barrier, inc=1, device_id=neighbour, device_id_type=MESH)
    pl.semaphore_wait(barrier, dp_size + vocab_size - 1)

    corner = vocab_size == 4
    direct = (1, 2) if corner else tuple(range(1, vocab_size))
    teacher_part = (th, t_send, t_recv)
    student_part = (sh, s_send, s_recv)
    for source, (held, send_sem, recv_sem) in ((th_ref, teacher_part), (sh_ref, student_part)):
        for k in range(1, dp_size):
            send(
                source, held.at[vocab, dp], send_sem.at[0, k], recv_sem.at[vocab, dp],
                (role, dps[k], vocab),
            )
        for k in direct:
            send(
                source, held.at[vocab, dp], send_sem.at[k, 0], recv_sem.at[vocab, dp],
                (role, dp, vocabs[k]),
            )

    targets_copy.wait()
    target_col[...] = jnp.transpose(jnp.broadcast_to(targets[...], (LANES, rows)))

    def pass_on(part, j):
        held, send_sem, recv_sem = part
        slot = held.at[vocab, dps[j]]
        arrived(slot, send_sem.at[0, 0], recv_sem.at[vocab, dps[j]])
        for k in direct:
            send(
                slot, slot, send_sem.at[k, j], recv_sem.at[vocab, dps[j]],
                (role, dp, vocabs[k]),
            )

    def relay(part, j):
        if not corner:
            return
        held, send_sem, recv_sem = part
        middle = block_rows // 2
        for k, at in ((1, pl.ds(0, middle)), (2, pl.ds(middle, middle))):
            slot = (vocabs[k], dps[j])
            arrived(held.at[slot], send_sem.at[0, 0], recv_sem.at[slot])
            piece = held.at[slot[0], slot[1], at]
            send(
                piece, piece, send_sem.at[vocab_size + k - 1, j], recv_sem.at[slot],
                (role, dp, vocabs[3 - k]),
            )

    def add_product(held, weights, acc, k):
        depth = held.shape[-1]
        start = pl.multiple_of(vocabs[k] * depth, 16)

        @pl.loop(0, cols // TILE)
        def _(n):
            at = pl.ds(pl.multiple_of(n * TILE, TILE), TILE)
            product = jnp.dot(
                held[vocabs[k]].reshape(rows, depth),
                weights[pl.ds(start, depth), at],
                preferred_element_type=jnp.float32,
            )
            if k == 0:
                acc[:, at] = product
            else:
                acc[:, at] += product

    def add_arriving(part, weights, acc, ks):
        held, send_sem, recv_sem = part
        for k in ks:
            if k == 3 or not corner:
                for j in range(dp_size):
                    slot = (vocabs[k], dps[j])
                    arrived(held.at[slot], send_sem.at[0, 0], recv_sem.at[slot])
            add_product(held, weights, acc, k)

    own_rows = pl.multiple_of(role * half, ROW_STEP)
    other_rows = pl.multiple_of((1 - role) * half, ROW_STEP)

    early, late = ((1, 2), (3,)) if corner else ((), direct)
    pass_on(teacher_part, 1)
    relay(teacher_part, 0)
    for j in range(2, dp_size):
        pass_on(teacher_part, j)
    relay(student_part, 0)
    pass_on(student_part, 1)
    for j in range(1, dp_size):
        relay(teacher_part, j)
        if j + 1 < dp_size:
            pass_on(student_part, j + 1)
    th_copy.wait()
    tw_copy.wait()
    add_product(th, tw, t_acc, 0)
    for j in range(1, dp_size):
        relay(student_part, j)
    sh_copy.wait()
    sw_copy.wait()
    add_arriving(teacher_part, tw, t_acc, early)
    add_product(sh, sw, s_acc, 0)
    add_arriving(student_part, sw, s_acc, early)
    add_arriving(teacher_part, tw, t_acc, late)
    send(t_acc.at[pl.ds(other_rows, half)], t_other, role_send.at[0], role_recv.at[0], partner)
    add_arriving(student_part, sw, s_acc, late)
    send(s_acc.at[pl.ds(other_rows, half)], s_other, role_send.at[1], role_recv.at[1], partner)
    arrived(t_other, role_send.at[0], role_recv.at[0])
    arrived(s_other, role_send.at[1], role_recv.at[1])

    column = lax.broadcasted_iota(jnp.int32, (ROW_STEP, cols), 1) + me * cols
    lane = lax.broadcasted_iota(jnp.int32, (ROW_STEP, LANES), 1)

    def at_rows(step):
        local = pl.ds(pl.multiple_of(step * ROW_STEP, ROW_STEP), ROW_STEP)
        whole = pl.ds(pl.multiple_of(own_rows + step * ROW_STEP, ROW_STEP), ROW_STEP)
        return local, whole

    @pl.loop(0, half // ROW_STEP)
    def _(step):
        local, whole = at_rows(step)
        teacher = t_acc[whole, :] + t_other[local, :]
        student = s_acc[whole, :] + s_other[local, :]
        hit = column == target_col[whole, 0:1]
        t_top = jnp.max(teacher, axis=1, keepdims=True)
        s_top = jnp.max(student, axis=1, keepdims=True)
        t_exp = jnp.exp(teacher - t_top)
        t_sum = jnp.sum(t_exp, axis=1, keepdims=True)
        gap = jnp.sum(t_exp * (teacher - student), axis=1, keepdims=True)
        s_sum = jnp.sum(jnp.exp(student - s_top), axis=1, keepdims=True)
        label = jnp.sum(jnp.where(hit, student, 0.0), axis=1, keepdims=True)
        packed = jnp.zeros((ROW_STEP, LANES), jnp.float32)
        for place, value in enumerate((t_top, t_sum, gap, s_top, s_sum, label)):
            packed = jnp.where(lane == place, value, packed)
        stat_col[local, :] = packed

    stats[me] = jnp.transpose(stat_col[...])[0:8, :]

    def stat_copy(step):
        other = lax.rem(me + step, group)
        return pltpu.make_async_remote_copy(
            src_ref=stats.at[me], dst_ref=stats.at[me],
            send_sem=stat_send.at[step], recv_sem=stat_recv.at[me],
            device_id=(role, lax.div(other, vocab_size), lax.rem(other, vocab_size)),
            device_id_type=MESH,
        )

    @pl.loop(1, group)
    def _(step):
        stat_copy(step).start()

    @pl.loop(1, group)
    def _(step):
        other = lax.rem(me + step, group)
        arrived(stats.at[other], stat_send.at[0], stat_recv.at[other])

    everyone = stats[...]
    t_top, t_sum, gap = everyone[:, 0, :], everyone[:, 1, :], everyone[:, 2, :]
    s_top, s_sum, label = everyone[:, 3, :], everyone[:, 4, :], everyone[:, 5, :]
    t_max = jnp.max(t_top, axis=0, keepdims=True)
    s_max = jnp.max(s_top, axis=0, keepdims=True)
    t_scale = jnp.exp(t_top - t_max)
    t_total = jnp.sum(t_sum * t_scale, axis=0, keepdims=True)
    s_total = jnp.sum(s_sum * jnp.exp(s_top - s_max), axis=0, keepdims=True)
    t_lse = t_max + jnp.log(t_total)
    s_lse = s_max + jnp.log(s_total)
    mean_gap = jnp.sum(gap * t_scale, axis=0, keepdims=True) / t_total
    s_label = jnp.sum(label, axis=0, keepdims=True)
    loss = (mean_gap - t_lse + s_lse) - (s_label - s_lse)
    losses[role] = jnp.broadcast_to(loss, (8, half))
    send(losses.at[role], losses.at[role], role_send.at[2], role_recv.at[2], partner)
    first = lax.broadcasted_iota(jnp.int32, (LANES, half), 0) == 0
    lse_col[...] = jnp.transpose(jnp.where(first, t_lse, s_lse))

    steps = half // ROW_STEP // 2
    part_rows = steps * ROW_STEP

    def grad_part(start, part):
        return logit_grad.at[pl.ds(pl.multiple_of(start + part * part_rows, ROW_STEP), part_rows)]

    for part in (0, 1):
        @pl.loop(part * steps, (part + 1) * steps)
        def _(step):
            local, whole = at_rows(step)
            teacher = t_acc[whole, :] + t_other[local, :]
            student = s_acc[whole, :] + s_other[local, :]
            onehot = jnp.where(column == target_col[whole, 0:1], 1.0, 0.0)
            t_prob = jnp.exp(teacher - lse_col[local, 0:1])
            s_prob = jnp.exp(student - lse_col[local, 1:2])
            logit_grad[whole, :] = (2.0 * s_prob - t_prob - onehot).astype(jnp.bfloat16)

        mine = grad_part(own_rows, part)
        send(mine, mine, role_send.at[3 + part], role_recv.at[3 + part], partner)
    for part in (0, 1):
        arrived(grad_part(other_rows, part), role_send.at[0], role_recv.at[3 + part])

    def block(j):
        return pl.ds(pl.multiple_of(dps[j] * block_rows, block_rows), block_rows)

    def send_term(k, j):
        send(
            term.at[k, block(j)], from_vocab.at[k, block(j)],
            v_send.at[k, j], v_recv.at[k, dps[j]], (role, dp, vocabs[k]),
        )

    far = list(range(dp_size - 1, -1, -1))

    def product(k, n, width):
        start = pl.multiple_of(vocabs[k] * features + n * width, width)
        return lax.dot_general(
            logit_grad[...], sw[pl.ds(start, width), :],
            (((1,), (1,)), ((), ())), preferred_element_type=jnp.float32,
        )

    def finish(j, total):
        to_dp[j] = total
        if j:
            send(to_dp.at[j], from_dp.at[j], d_send.at[j], d_recv.at[j], (role, dps[j], vocab))

    if corner:
        width = features // 2
        sides = (pl.ds(0, width), pl.ds(width, width))

        def hop(side, slot, j):
            send(
                out_hop.at[side, slot, block(j)], in_hop.at[side, slot, block(j)],
                h_send.at[side, slot, j], h_recv.at[side, slot, dps[j]],
                (role, dp, vocabs[1 + side]),
            )

        def landed(buffer, side, slot, j):
            arrived(
                buffer.at[side, slot, block(j)] if slot < 2 else buffer.at[side, block(j)],
                h_send.at[0, 0, 0], h_recv.at[side, slot, dps[j]],
            )

        def sum_middle(j):
            for side in (0, 1):
                landed(in_hop, side, 1, j)
                middle[side, block(j)] += in_hop[side, 1, block(j)].astype(jnp.float32)
                send(
                    middle.at[side, block(j)], in_last.at[side, block(j)],
                    h_send.at[side, 2, j], h_recv.at[side, 2, dps[j]],
                    (role, dp, vocabs[2 - side]),
                )

        def sum_last(j):
            totals = []
            for side in (0, 1):
                landed(in_hop, side, 0, j)
                near = term[0, block(j), sides[side]] + in_hop[side, 0, block(j)].astype(jnp.float32)
                landed(in_last, side, 2, j)
                totals.append(near + in_last[side, block(j)])
            finish(j, jnp.concatenate(totals, axis=1))

        for side in (0, 1):
            out_hop[side, 1] = product(3, side, width).astype(HOP)
            hop(side, 1, far[0])
        for side in (0, 1):
            out_hop[side, 0] = product(1 + side, side, width).astype(HOP)
            hop(side, 0, far[0])
            for j in far[1:2]:
                hop(side, 1, j)
        for side in (0, 1):
            middle[side] = product(2 - side, side, width)
        for side in (0, 1):
            term[0, :, sides[side]] = product(0, side, width)
        for at, j in enumerate(far):
            sum_middle(j)
            for side in (0, 1):
                for later in far[at + 1:at + 2]:
                    hop(side, 0, later)
                for later in far[at + 2:at + 3]:
                    hop(side, 1, later)
            if at:
                sum_last(far[at - 1])
        sum_last(far[-1])
    else:
        width = min(TILE, features)
        order = list(range(vocab_size - 1, -1, -1))
        for k in order:
            @pl.loop(0, features // width)
            def _(n):
                term[k, :, pl.ds(pl.multiple_of(n * width, width), width)] = product(k, n, width)
            if k:
                send_term(k, far[0])
        for j in far[1:]:
            for k in order[:-1]:
                send_term(k, j)
        for j in far:
            total = term[0, block(j), :]
            for k in order[:-1]:
                arrived(from_vocab.at[k, block(j)], v_send.at[0, 0], v_recv.at[k, dps[j]])
                total = total + from_vocab[k, block(j), :]
            finish(j, total)
    result = to_dp[0]
    for j in far[:-1]:
        arrived(from_dp.at[j], d_send.at[0], d_recv.at[j])
        result = result + from_dp[j]
    grad_ref[...] = result

    arrived(losses.at[1 - role], role_send.at[2], role_recv.at[2])
    both = losses[:, 0, :]
    loss_ref[:, 0:half] = both[0:1]
    loss_ref[:, half:rows] = both[1:2]
    mean_ref[...] = jnp.sum(jnp.sum(both, axis=1, keepdims=True), axis=0, keepdims=True) * (1.0 / rows)

    for copy in sent:
        copy.wait_send()

    @pl.loop(1, group)
    def _(step):
        stat_copy(step).wait_send()


def per_device(dp_size, vocab_size, teacher_hidden, student_hidden, teacher_unembed, student_unembed, targets):
    block_rows, t_depth = teacher_hidden.shape
    s_depth = student_hidden.shape[1]
    rows = dp_size * block_rows
    half = rows // 2
    cols = teacher_unembed.shape[1]
    group = dp_size * vocab_size
    corner = vocab_size == 4
    hop_rows = rows if corner else 16
    f32, bf16 = jnp.float32, jnp.bfloat16
    vmem, dma = pltpu.VMEM, pltpu.SemaphoreType.DMA
    any_spec = pl.BlockSpec(memory_space=pltpu.HBM)
    vmem_spec = pl.BlockSpec(memory_space=pltpu.VMEM)
    losses, mean, grad = pl.pallas_call(
        functools.partial(kernel, dp_size, vocab_size),
        out_shape=(
            jax.ShapeDtypeStruct((1, rows), f32),
            jax.ShapeDtypeStruct((1, 1), f32),
            jax.ShapeDtypeStruct((block_rows, s_depth), f32),
        ),
        in_specs=[any_spec] * 5,
        out_specs=(vmem_spec,) * 3,
        scratch_shapes=[
            vmem((vocab_size, dp_size, block_rows, t_depth), bf16),
            vmem((vocab_size, dp_size, block_rows, s_depth), bf16),
            vmem(teacher_unembed.shape, bf16),
            vmem(student_unembed.shape, bf16),
            vmem((1, rows), jnp.int32),
            vmem((rows, cols), f32),
            vmem((rows, cols), f32),
            vmem((half, cols), f32),
            vmem((half, cols), f32),
            vmem((rows, LANES), jnp.int32),
            vmem((half, LANES), f32),
            vmem((group, 8, half), f32),
            vmem((2, 8, half), f32),
            vmem((half, LANES), f32),
            vmem((rows, cols), bf16),
            vmem((1 if corner else vocab_size, rows, s_depth), f32),
            vmem((1 if corner else vocab_size, 8 if corner else rows, s_depth), f32),
            vmem((2, 2, hop_rows, s_depth // 2), HOP),
            vmem((2, 2, hop_rows, s_depth // 2), HOP),
            vmem((2, hop_rows, s_depth // 2), f32),
            vmem((2, hop_rows, s_depth // 2), f32),
            vmem((dp_size, block_rows, s_depth), f32),
            vmem((dp_size, block_rows, s_depth), f32),
            dma((5,)),
            dma((vocab_size + 2, dp_size)),
            dma((vocab_size, dp_size)),
            dma((vocab_size + 2, dp_size)),
            dma((vocab_size, dp_size)),
            dma((5,)),
            dma((5,)),
            dma((group,)),
            dma((group,)),
            dma((vocab_size, dp_size)),
            dma((vocab_size, dp_size)),
            dma((2, 3, dp_size)),
            dma((2, 3, dp_size)),
            dma((dp_size,)),
            dma((dp_size,)),
        ],
        compiler_params=pltpu.CompilerParams(
            collective_id=0, has_side_effects=True, vmem_limit_bytes=50 * 1024 * 1024
        ),
    )(teacher_hidden, student_hidden, teacher_unembed, student_unembed, targets.reshape(1, rows))
    return losses.reshape(rows), mean.reshape(()), grad


def solution(mesh):
    return jax.shard_map(
        functools.partial(per_device, mesh.shape["dp"], mesh.shape["vocab"]),
        mesh=mesh,
        in_specs=(
            P("dp", ("role", "vocab")),
            P("dp", ("role", "vocab")),
            P("role", ("dp", "vocab")),
            P("role", ("dp", "vocab")),
            P(),
        ),
        out_specs=(P(), P(), P("dp", ("role", "vocab"))),
        check_vma=False,
    )
```
